32 devices in a mesh: ta: 8 (over z, x), ba: 4 (over y, core).
Axes of the slice: x: 2, y: 2, z: 4, core: 2. Of those that a mesh axis runs over, the one named last changes fastest.
Arguments:
- samples: int32 [262144, 512], P('ta', 'ba'), may hold values from -128 to 127
- input_gain: float32 [512], P('ba'), may hold values from 0.005 to 0.03
- pfb_weights: float32 [16, 1024], replicated, may hold values from -1.5 to 1.5
- chan_map: int32 [512], replicated, may hold values from 0 to 511, each once
Outputs:
- visibility: float32 [2, 512, 512, 512], P(None, ('ta', 'ba'))
The draws below stay inside these ranges and needn't reach their ends.
Inputs may be any that keep to these rules, and one draw needn't show every extreme that they name: `chan_map`: each of the 512 channel numbers appears exactly once.
All inputs are finite; a program needn't handle non-finite values.
Results may differ from the reference program's by a relative error of at most 0.0036.
Values may be sent and summed in bfloat16 or wider, within the bound.
A program may use at most 192 MiB of HBM per device.

```python
import math
import jax
import jax.numpy as jnp
from jax import lax

INPUTS = 512
CHANNELS = 512
TAPS = 16
FRAME = 1024
SPECTRA = 256
SAMPLES = 262144


def with_ends(values, key, least, top_value):
    dims = values.shape
    place = [jax.random.randint(jax.random.fold_in(key, axis), (), 0, dims[axis]) for axis in range(len(dims))]
    values = values.at[tuple(place)].set(least)
    longest = dims.index(max(dims))
    place[longest] = (place[longest] + 1) % dims[longest]
    return values.at[tuple(place)].set(top_value)


def block_scale(stream_key, dims, split, least, largest):
    factor_of, own = 1.0, jax.random.fold_in(stream_key, 6)
    for position, parts in split:
        steps = jnp.exp(jax.random.uniform(jax.random.fold_in(own, position), (parts,), jnp.float32, least / len(split), largest / len(split)))
        factor_of = factor_of * jnp.repeat(steps, dims[position] // parts).reshape([-1 if axis == position else 1 for axis in range(len(dims))])
    return factor_of


def scatter_about(own_key, shape, deviation, reach, held_as=jnp.bfloat16):
    return jnp.clip(deviation * jax.random.normal(own_key, shape, jnp.float32), -reach, reach).astype(held_as)


def setup_inputs(seed: int = 0) -> dict:
    streams_of = jax.random.split(jax.random.key(seed), 5)
    samples = with_ends(jax.random.randint(streams_of[0], (SAMPLES, INPUTS), -128, 128), jax.random.fold_in(streams_of[0], 1), -128, 127).astype(jnp.int32)
    input_gain = jnp.clip(jnp.exp(math.log(0.03) - 1.7917595 * jax.random.uniform(streams_of[1], (INPUTS,), jnp.float32) ** block_scale(streams_of[1], (INPUTS,), ((0, 4),), -0.2, 0.2)), 0.005, 0.03)
    pfb_weights = scatter_about(streams_of[2], (TAPS, FRAME), TAPS ** -0.5, 1.5, jnp.float32)
    chan_map = jax.random.permutation(streams_of[3], CHANNELS).astype(jnp.int32)
    return {"samples": samples, "input_gain": input_gain, "pfb_weights": pfb_weights, "chan_map": chan_map}


def build_table(chan_map, frame_len):
    sample_idx = jnp.arange(frame_len, dtype=jnp.int32)
    product = sample_idx[:, None] * chan_map[None, :].astype(jnp.int32) % frame_len
    angle = product.astype(jnp.float32) * (2.0 * math.pi / frame_len)
    scale = 1.0 / math.sqrt(frame_len)
    stacked = jnp.stack([jnp.cos(angle) * scale, -jnp.sin(angle) * scale], axis=-1)
    return stacked.reshape(frame_len, -1).astype(jnp.bfloat16)

def reference(samples, input_gain, pfb_weights, chan_map):
    dft_table = build_table(chan_map, FRAME)
    block_width = min(128, INPUTS)
    pieces = []
    for start in range(0, INPUTS, block_width):
        raw = samples[:, start:start + block_width].astype(jnp.float32)
        calibrated = (raw * input_gain[None, start:start + block_width]).astype(jnp.bfloat16)
        frames = calibrated.reshape(SPECTRA, FRAME, block_width)
        extended = jnp.concatenate([jnp.zeros((TAPS - 1, FRAME, block_width), jnp.bfloat16), frames], axis=0)
        running = jnp.zeros((SPECTRA, FRAME, block_width), jnp.float32)
        for tap_index in range(TAPS):
            running = running + pfb_weights[tap_index][None, :, None] * extended[tap_index:tap_index + SPECTRA].astype(jnp.float32)
        filtered = running.astype(jnp.bfloat16)
        spectra = jnp.einsum('sni,nk->sik', filtered.astype(jnp.float32), dft_table.astype(jnp.float32))
        pieces.append(spectra.astype(jnp.bfloat16))
    spectra = jnp.concatenate(pieces, axis=1)
    group = 4 if CHANNELS % 4 == 0 else 1
    grouped = spectra.reshape(SPECTRA, INPUTS, CHANNELS // group, group, 2).transpose(2, 0, 1, 3, 4)

    def correlate(cells):
        values = cells.astype(jnp.float32)
        rotated = jnp.stack([values[..., 1], -values[..., 0]], axis=-1)
        stacked = jnp.stack([values, rotated], axis=0)
        return jnp.einsum('osicp,sjcp->ocij', stacked, values) / SPECTRA
    result = lax.map(correlate, grouped)
    return result.transpose(1, 0, 2, 3, 4).reshape(2, CHANNELS, INPUTS, INPUTS)
```

```python
import functools
import math

import jax
import jax.numpy as jnp
from jax import lax
from jax.experimental import pallas as pl
from jax.experimental.pallas import tpu as pltpu
from jax.sharding import PartitionSpec as P

MESH = pl.DeviceIdType.MESH
CHUNK = 16
ROWS = 256


def table_factors(chan_map, frame_len):
    chan = jnp.repeat(chan_map, 2)
    quarter = jnp.tile(jnp.array([0, frame_len // 4], jnp.int32), chan_map.shape[0])
    step = 2.0 * math.pi / frame_len
    blocks = jnp.arange(frame_len // 128, dtype=jnp.int32) * 128
    lanes = jnp.arange(128, dtype=jnp.int32)
    coarse = ((chan[:, None] * blocks[None, :] + quarter[:, None]) % frame_len).astype(jnp.float32) * step
    fine = (chan[:, None] * lanes[None, :] % frame_len).astype(jnp.float32) * step
    scale = 1.0 / math.sqrt(frame_len)
    coarse_pair = jnp.concatenate([jnp.cos(coarse) * scale, jnp.sin(coarse) * scale], axis=1)
    return coarse_pair, jnp.cos(fine), jnp.sin(fine)


def turn_kernel(
    shape, samples, gain, weights, coarse, fine_cos, fine_sin, received,
    raw, cal, filtered, table, partial, spectra,
    load_sem, halo_send, halo_recv, send_sem, recv_sem, own_sem,
):
    n_ta, n_ba, taps, frames, frame_len = shape
    n_dev = n_ta * n_ba
    halo = taps - 1
    ta, ba = lax.axis_index("ta"), lax.axis_index("ba")
    me = ta * n_ba + ba
    table_rows = table.shape[0]
    rows_dev = table_rows // n_dev
    blocks = table_rows // ROWS
    dests = n_dev // blocks

    late = pltpu.make_async_copy(samples.at[pl.ds(frames - halo, halo)], raw.at[pl.ds(frames - halo, halo)], load_sem.at[0])
    early = pltpu.make_async_copy(samples.at[pl.ds(0, frames - halo)], raw.at[pl.ds(0, frames - halo)], load_sem.at[1])
    late.start()
    early.start()

    barrier = pltpu.get_barrier_semaphore()

    @pl.loop(1, n_dev)
    def _(step):
        other = lax.rem(me + step, n_dev)
        pl.semaphore_signal(
            barrier, inc=1, device_id=(other // n_ba, lax.rem(other, n_ba)), device_id_type=MESH
        )

    def calibrate(first, count):
        pieces = frame_len // 128

        @pl.loop(0, count * pieces)
        def _(step):
            frame = first + step // pieces
            rows = pl.ds(pl.multiple_of(lax.rem(step, pieces) * 128, 128), 128)
            value = raw[frame, rows, :].astype(jnp.float32) * gain[...]
            cal[frame + halo, rows, :] = value.astype(jnp.bfloat16)

    late.wait()
    calibrate(frames - halo, halo)
    pl.semaphore_wait(barrier, n_dev - 1)

    halo_copy = pltpu.make_async_remote_copy(
        src_ref=cal.at[pl.ds(frames, halo)],
        dst_ref=cal.at[pl.ds(0, halo)],
        send_sem=halo_send,
        recv_sem=halo_recv,
        device_id=(jnp.minimum(ta + 1, n_ta - 1), ba),
        device_id_type=MESH,
    )

    @pl.when(ta < n_ta - 1)
    def _():
        halo_copy.start()

    for a in range(frame_len // 128):
        cos_a = coarse[:, a : a + 1]
        sin_a = coarse[:, a + frame_len // 128 : a + frame_len // 128 + 1]
        table[:, a * 128 : (a + 1) * 128] = (fine_cos[...] * cos_a - fine_sin[...] * sin_a).astype(jnp.bfloat16)

    early.wait()
    calibrate(0, frames - halo)

    lower = 1 - ta // (n_ta // 2)

    def message(q, dest):
        return pltpu.make_async_remote_copy(
            src_ref=spectra.at[q, pl.ds(dest * rows_dev, rows_dev)],
            dst_ref=received.at[q, me],
            send_sem=send_sem.at[q, dest],
            recv_sem=recv_sem.at[q, me],
            device_id=(dest // n_ba, lax.rem(dest, n_ba)),
            device_id_type=MESH,
        )

    def own(q):
        return pltpu.make_async_copy(
            spectra.at[q, pl.ds(me * rows_dev, rows_dev)], received.at[q, me], own_sem.at[q]
        )

    n_chunks = frames // CHUNK

    @pl.loop(0, n_chunks)
    def _(chunk):
        q = n_chunks - 1 - chunk

        @pl.when(jnp.logical_and(chunk == n_chunks - 1, ta > 0))
        def _():
            halo_copy.wait_recv()

        @pl.when(jnp.logical_and(chunk == n_chunks - 1, ta == 0))
        def _():
            @pl.loop(0, halo)
            def _(frame):
                cal[frame] = jnp.zeros((frame_len, 128), jnp.bfloat16)

        @pl.loop(0, frame_len // 16)
        def _(block):
            rows = pl.ds(pl.multiple_of(block * 16, 16), 16)
            own_weights = weights[rows, :]
            taps_here = [jnp.broadcast_to(own_weights[:, t : t + 1], (16, 128)) for t in range(taps)]
            for group in range(CHUNK // 4):
                sums = [None] * 4
                for f in range(taps + 3):
                    x = cal[q * CHUNK + group * 4 + f, rows, :].astype(jnp.float32)
                    for j in range(4):
                        t = f - j
                        if 0 <= t < taps:
                            term = taps_here[t] * x
                            sums[j] = term if sums[j] is None else sums[j] + term
                for j in range(4):
                    s = group * 4 + j
                    filtered[s // 2, rows, (s % 2) * 128 : (s % 2 + 1) * 128] = sums[j].astype(jnp.bfloat16)

        @pl.loop(0, blocks)
        def _(p):
            b = p + (blocks - 1 - 2 * p) * lower
            base = pl.multiple_of(b * ROWS, ROWS)
            left = table[pl.ds(base, ROWS), :]

            @pl.loop(0, CHUNK // 2)
            def _(pair):
                result = jnp.dot(left, filtered[pair], preferred_element_type=jnp.float32)
                start = pl.multiple_of(pair * 2 * ROWS, ROWS)
                partial[pl.ds(start, ROWS), :] = result[:, :128]
                partial[pl.ds(start + ROWS, ROWS), :] = result[:, 128:]

            @pl.loop(0, ROWS // 8)
            def _(k8):
                for r in range(8):
                    k = k8 * 8 + r
                    spectra[q, base + k] = partial[pl.ds(k, CHUNK, stride=ROWS), :].astype(jnp.bfloat16)

            @pl.loop(0, dests)
            def _(j):
                dest = b * dests + lax.rem(j + me, dests)

                @pl.when(dest != me)
                def _():
                    message(q, dest).start()

                @pl.when(dest == me)
                def _():
                    own(q).start()

    @pl.when(ta < n_ta - 1)
    def _():
        halo_copy.wait_send()

    @pl.loop(0, n_chunks)
    def _(q):
        own(q).wait()

        @pl.loop(1, n_dev)
        def _(step):
            other = lax.rem(me + step, n_dev)
            message(q, other).wait_send()
            pltpu.make_async_remote_copy(
                src_ref=spectra.at[q, pl.ds(other * rows_dev, rows_dev)],
                dst_ref=received.at[q, other],
                send_sem=send_sem.at[q, other],
                recv_sem=recv_sem.at[q, other],
                device_id=(other // n_ba, lax.rem(other, n_ba)),
                device_id_type=MESH,
            ).wait_recv()


def correlate_kernel(scale, received, out):
    n_chunks, n_ta, n_ba = received.shape[:3]
    depth = n_chunks * n_ta * received.shape[4]

    def part(p):
        return jnp.concatenate(
            [received[:, :, b, p].reshape(depth, 128) for b in range(n_ba)], axis=1
        )

    re, im = part(0), part(1)
    right = jnp.concatenate([re, im], axis=0)
    re_t, im_t = re.T, im.T
    out[0, 0] = jnp.dot(jnp.concatenate([re_t, im_t], axis=1), right, preferred_element_type=jnp.float32) * scale
    out[1, 0] = jnp.dot(jnp.concatenate([im_t, -re_t], axis=1), right, preferred_element_type=jnp.float32) * scale


def per_device(samples, input_gain, pfb_weights, chan_map):
    taps, frame_len = pfb_weights.shape
    frames = samples.shape[0] // frame_len
    n_ta, n_ba = lax.axis_size("ta"), lax.axis_size("ba")
    n_dev = n_ta * n_ba
    table_rows = 2 * chan_map.shape[0]
    rows_dev = table_rows // n_dev
    n_chunks = frames // CHUNK
    inputs = n_ba * samples.shape[1]
    coarse, fine_cos, fine_sin = table_factors(chan_map, frame_len)
    vmem = pl.BlockSpec(memory_space=pltpu.VMEM)
    hbm = pl.BlockSpec(memory_space=pl.ANY)
    received = pl.pallas_call(
        functools.partial(turn_kernel, (n_ta, n_ba, taps, frames, frame_len)),
        out_shape=jax.ShapeDtypeStruct((n_chunks, n_dev, rows_dev, CHUNK, 128), jnp.bfloat16),
        in_specs=[hbm, vmem, vmem, vmem, vmem, vmem],
        out_specs=hbm,
        scratch_shapes=[
            pltpu.VMEM((frames, frame_len, 128), jnp.int32),
            pltpu.VMEM((frames + taps - 1, frame_len, 128), jnp.bfloat16),
            pltpu.VMEM((CHUNK // 2, frame_len, 256), jnp.bfloat16),
            pltpu.VMEM((table_rows, frame_len), jnp.bfloat16),
            pltpu.VMEM((CHUNK * ROWS, 128), jnp.float32),
            pltpu.VMEM((n_chunks, table_rows, CHUNK, 128), jnp.bfloat16),
            pltpu.SemaphoreType.DMA((2,)),
            pltpu.SemaphoreType.DMA,
            pltpu.SemaphoreType.DMA,
            pltpu.SemaphoreType.DMA((n_chunks, n_dev)),
            pltpu.SemaphoreType.DMA((n_chunks, n_dev)),
            pltpu.SemaphoreType.DMA((n_chunks,)),
        ],
        compiler_params=pltpu.CompilerParams(
            collective_id=0, has_side_effects=True, vmem_limit_bytes=56 * 1024 * 1024
        ),
        name="filter_turn",
    )(samples.reshape(frames, frame_len, 128), input_gain[None, :], pfb_weights.T, coarse, fine_cos, fine_sin)
    received = received.reshape(n_chunks, n_ta, n_ba, rows_dev, CHUNK, 128)
    channels_dev = rows_dev // 2
    return pl.pallas_call(
        functools.partial(correlate_kernel, 1.0 / (n_ta * frames)),
        grid=(channels_dev,),
        out_shape=jax.ShapeDtypeStruct((2, channels_dev, inputs, inputs), jnp.float32),
        in_specs=[pl.BlockSpec((n_chunks, n_ta, n_ba, 2, CHUNK, 128), lambda c: (0, 0, 0, c, 0, 0))],
        out_specs=pl.BlockSpec((2, 1, inputs, inputs), lambda c: (0, c, 0, 0)),
        compiler_params=pltpu.CompilerParams(vmem_limit_bytes=48 * 1024 * 1024),
        name="correlate",
    )(received)


def solution(mesh):
    placed = (P("ta", "ba"), P("ba"), P(), P())
    return jax.shard_map(
        per_device,
        mesh=mesh,
        in_specs=placed,
        out_specs=P(None, ("ta", "ba"), None, None),
        check_vma=False,
    )
```

```python
import functools
import math

import jax
import jax.numpy as jnp
from jax import lax
from jax.experimental import pallas as pl
from jax.experimental.pallas import tpu as pltpu
from jax.sharding import PartitionSpec as P

MESH = pl.DeviceIdType.MESH
CHUNK = 16
ROWS = 256


def turn_kernel(
    shape, samples, gain, pfb_weights, chan_map, received,
    raw, cal, weights, filtered, table, partial, spectra,
    load_sem, halo_send, halo_recv, send_sem, recv_sem, own_sem,
):
    n_ta, n_ba, taps, frames, frame_len = shape
    n_dev = n_ta * n_ba
    half = CHUNK // 2
    before, after = taps - 1 - half, half
    ta, ba = lax.axis_index("ta"), lax.axis_index("ba")
    me = ta * n_ba + ba
    table_rows = table.shape[0]
    rows_dev = table_rows // n_dev
    blocks = table_rows // ROWS
    dests = n_dev // blocks

    def load(index, first, count):
        return pltpu.make_async_copy(
            samples.at[pl.ds(first, count)], raw.at[pl.ds(first, count)], load_sem.at[index]
        )

    last = load(0, frames - before, before)
    first = load(1, 0, after)
    middle = load(2, after, frames - before - after)
    last.start()
    first.start()
    middle.start()

    barrier = pltpu.get_barrier_semaphore()

    @pl.loop(1, n_dev)
    def _(step):
        other = lax.rem(me + step, n_dev)
        pl.semaphore_signal(
            barrier, inc=1, device_id=(other // n_ba, lax.rem(other, n_ba)), device_id_type=MESH
        )

    def calibrate(start, count):
        pieces = frame_len // 256

        @pl.loop(0, count * pieces)
        def _(step):
            frame = start + step // pieces
            rows = pl.ds(pl.multiple_of(lax.rem(step, pieces) * 256, 256), 256)
            value = raw[frame, rows, :].astype(jnp.float32) * gain[...]
            cal[frame + before, rows, :] = value.astype(jnp.bfloat16)

    forward = pltpu.make_async_remote_copy(
        src_ref=cal.at[pl.ds(frames, before)],
        dst_ref=cal.at[pl.ds(0, before)],
        send_sem=halo_send.at[0],
        recv_sem=halo_recv.at[0],
        device_id=(jnp.minimum(ta + 1, n_ta - 1), ba),
        device_id_type=MESH,
    )
    backward = pltpu.make_async_remote_copy(
        src_ref=cal.at[pl.ds(before, after)],
        dst_ref=cal.at[pl.ds(before + frames, after)],
        send_sem=halo_send.at[1],
        recv_sem=halo_recv.at[1],
        device_id=(lax.rem(ta + n_ta - 1, n_ta), ba),
        device_id_type=MESH,
    )

    last.wait()
    calibrate(frames - before, before)
    pl.semaphore_wait(barrier, n_dev - 1)

    @pl.when(ta < n_ta - 1)
    def _():
        forward.start()

    first.wait()
    calibrate(0, after)
    backward.start()
    middle.wait()
    calibrate(after, frames - before - after)

    filler = jnp.zeros((128 - taps, frame_len), jnp.float32)
    weights[...] = jnp.concatenate([pfb_weights[...], filler], axis=0).T

    step_angle = 2.0 * math.pi / frame_len
    scale = 1.0 / math.sqrt(frame_len)
    chans = ROWS // 2

    def pair(turns):
        centred = ((turns + frame_len // 2) & (frame_len - 1)) - frame_len // 2
        angle = centred.astype(jnp.float32) * step_angle
        return jnp.cos(angle), jnp.sin(angle)

    lane = lax.broadcasted_iota(jnp.int32, (chans, 128), 1)
    for b in range(blocks):
        row = chan_map[:, b * chans : (b + 1) * chans].astype(jnp.float32)
        chan = jnp.broadcast_to(row, (128, chans)).T.astype(jnp.int32)
        fine_cos, fine_sin = pair(chan * lane)
        coarse_cos, coarse_sin = pair(chan * lane * 128)
        for a in range(frame_len // 128):
            cos_a = coarse_cos[:, a : a + 1] * scale
            sin_a = coarse_sin[:, a : a + 1] * scale
            columns = slice(a * 128, (a + 1) * 128)
            real = fine_cos * cos_a - fine_sin * sin_a
            imaginary = -(fine_sin * cos_a + fine_cos * sin_a)
            table[b * ROWS : b * ROWS + chans, columns] = real.astype(jnp.bfloat16)
            table[b * ROWS + chans : (b + 1) * ROWS, columns] = imaginary.astype(jnp.bfloat16)

    lower = 1 - ta // (n_ta // 2)

    def message(q, dest):
        return pltpu.make_async_remote_copy(
            src_ref=spectra.at[q, pl.ds(dest * rows_dev, rows_dev)],
            dst_ref=received.at[q, me],
            send_sem=send_sem.at[q, dest],
            recv_sem=recv_sem.at[q, me],
            device_id=(dest // n_ba, lax.rem(dest, n_ba)),
            device_id_type=MESH,
        )

    def own(q):
        return pltpu.make_async_copy(
            spectra.at[q, pl.ds(me * rows_dev, rows_dev)], received.at[q, me], own_sem.at[q]
        )

    @pl.loop(0, 2)
    def _(q):
        @pl.when(jnp.logical_and(q == 1, ta > 0))
        def _():
            forward.wait_recv()

        @pl.when(jnp.logical_and(q == 1, ta == 0))
        def _():
            @pl.loop(0, before)
            def _(frame):
                cal[frame] = jnp.zeros((frame_len, 128), jnp.bfloat16)

        @pl.when(q == 1)
        def _():
            backward.wait_recv()

        @pl.when(jnp.logical_and(q == 1, ta == n_ta - 1))
        def _():
            @pl.loop(frames + before - taps + 1, frames + before)
            def _(frame):
                cal[frame] = jnp.zeros((frame_len, 128), jnp.bfloat16)

        @pl.loop(0, frame_len // 16)
        def _(block):
            rows = pl.ds(pl.multiple_of(block * 16, 16), 16)
            own_weights = weights[rows, :]
            taps_here = [jnp.broadcast_to(own_weights[:, t : t + 1], (16, 128)) for t in range(taps)]
            for group in range(CHUNK // 4):
                side = group * 4 // half
                lead = (1 - q) * (half + side * half) + q * side * (frames - half) + group * 4 - side * half
                sums = [None] * 4
                for f in range(taps + 3):
                    x = cal[lead + f, rows, :].astype(jnp.float32)
                    for j in range(4):
                        t = f - j
                        if 0 <= t < taps:
                            term = taps_here[t] * x
                            sums[j] = term if sums[j] is None else sums[j] + term
                for j in range(4):
                    s = group * 4 + j
                    filtered[s // 2, rows, (s % 2) * 128 : (s % 2 + 1) * 128] = sums[j].astype(jnp.bfloat16)

        @pl.loop(0, blocks)
        def _(p):
            b = p + (blocks - 1 - 2 * p) * lower
            base = pl.multiple_of(b * ROWS, ROWS)
            left = table[pl.ds(base, ROWS), :]

            @pl.loop(0, CHUNK // 2)
            def _(two):
                result = jnp.dot(left, filtered[two], preferred_element_type=jnp.float32)
                start = pl.multiple_of(two * 2 * ROWS, ROWS)
                partial[pl.ds(start, ROWS), :] = result[:, :128]
                partial[pl.ds(start + ROWS, ROWS), :] = result[:, 128:]

            @pl.loop(0, chans // 8)
            def _(c8):
                for r in range(8):
                    c = c8 * 8 + r
                    for p in range(2):
                        values = partial[pl.ds(c + p * chans, CHUNK, stride=ROWS), :]
                        spectra[q, base + 2 * c + p] = values.astype(jnp.bfloat16)

            @pl.loop(0, dests)
            def _(j):
                dest = b * dests + lax.rem(j + me, dests)

                @pl.when(dest != me)
                def _():
                    message(q, dest).start()

                @pl.when(dest == me)
                def _():
                    own(q).start()

    @pl.when(ta < n_ta - 1)
    def _():
        forward.wait_send()

    backward.wait_send()

    @pl.loop(0, 2)
    def _(q):
        own(q).wait()

        @pl.loop(1, n_dev)
        def _(step):
            other = lax.rem(me + step, n_dev)
            message(q, other).wait_send()
            pltpu.make_async_remote_copy(
                src_ref=spectra.at[q, pl.ds(other * rows_dev, rows_dev)],
                dst_ref=received.at[q, other],
                send_sem=send_sem.at[q, other],
                recv_sem=recv_sem.at[q, other],
                device_id=(other // n_ba, lax.rem(other, n_ba)),
                device_id_type=MESH,
            ).wait_recv()


def correlate_kernel(scale, received, out):
    n_chunks, n_ta, n_ba = received.shape[:3]
    depth = n_chunks * n_ta * received.shape[4]

    def part(p):
        return jnp.concatenate(
            [received[:, :, b, p].reshape(depth, 128) for b in range(n_ba)], axis=1
        )

    re, im = part(0), part(1)
    right = jnp.concatenate([re, im], axis=0)
    re_t, im_t = re.T, im.T
    out[0, 0] = jnp.dot(jnp.concatenate([re_t, im_t], axis=1), right, preferred_element_type=jnp.float32) * scale
    out[1, 0] = jnp.dot(jnp.concatenate([im_t, -re_t], axis=1), right, preferred_element_type=jnp.float32) * scale


def per_device(samples, input_gain, pfb_weights, chan_map):
    taps, frame_len = pfb_weights.shape
    frames = samples.shape[0] // frame_len
    n_ta, n_ba = lax.axis_size("ta"), lax.axis_size("ba")
    n_dev = n_ta * n_ba
    table_rows = 2 * chan_map.shape[0]
    rows_dev = table_rows // n_dev
    n_chunks = frames // CHUNK
    inputs = n_ba * samples.shape[1]
    vmem = pl.BlockSpec(memory_space=pltpu.VMEM)
    hbm = pl.BlockSpec(memory_space=pl.ANY)
    received = pl.pallas_call(
        functools.partial(turn_kernel, (n_ta, n_ba, taps, frames, frame_len)),
        out_shape=jax.ShapeDtypeStruct((n_chunks, n_dev, rows_dev, CHUNK, 128), jnp.bfloat16),
        in_specs=[hbm, vmem, vmem, vmem],
        out_specs=hbm,
        scratch_shapes=[
            pltpu.VMEM((frames, frame_len, 128), jnp.int32),
            pltpu.VMEM((frames + taps - 1, frame_len, 128), jnp.bfloat16),
            pltpu.VMEM((frame_len, 128), jnp.float32),
            pltpu.VMEM((CHUNK // 2, frame_len, 256), jnp.bfloat16),
            pltpu.VMEM((table_rows, frame_len), jnp.bfloat16),
            pltpu.VMEM((CHUNK * ROWS, 128), jnp.float32),
            pltpu.VMEM((n_chunks, table_rows, CHUNK, 128), jnp.bfloat16),
            pltpu.SemaphoreType.DMA((3,)),
            pltpu.SemaphoreType.DMA((2,)),
            pltpu.SemaphoreType.DMA((2,)),
            pltpu.SemaphoreType.DMA((n_chunks, n_dev)),
            pltpu.SemaphoreType.DMA((n_chunks, n_dev)),
            pltpu.SemaphoreType.DMA((n_chunks,)),
        ],
        compiler_params=pltpu.CompilerParams(
            collective_id=0, has_side_effects=True, vmem_limit_bytes=56 * 1024 * 1024
        ),
        name="filter_turn",
    )(samples.reshape(frames, frame_len, 128), input_gain[None, :], pfb_weights, chan_map[None, :])
    received = received.reshape(n_chunks, n_ta, n_ba, rows_dev, CHUNK, 128)
    channels_dev = rows_dev // 2
    return pl.pallas_call(
        functools.partial(correlate_kernel, 1.0 / (n_ta * frames)),
        grid=(channels_dev,),
        out_shape=jax.ShapeDtypeStruct((2, channels_dev, inputs, inputs), jnp.float32),
        in_specs=[pl.BlockSpec((n_chunks, n_ta, n_ba, 2, CHUNK, 128), lambda c: (0, 0, 0, c, 0, 0))],
        out_specs=pl.BlockSpec((2, 1, inputs, inputs), lambda c: (0, c, 0, 0)),
        compiler_params=pltpu.CompilerParams(vmem_limit_bytes=48 * 1024 * 1024),
        name="correlate",
    )(received)


def solution(mesh):
    placed = (P("ta", "ba"), P("ba"), P(), P())
    return jax.shard_map(
        per_device,
        mesh=mesh,
        in_specs=placed,
        out_specs=P(None, ("ta", "ba"), None, None),
        check_vma=False,
    )
```

```python
import functools
import math

import jax
import jax.numpy as jnp
from jax import lax
from jax.experimental import pallas as pl
from jax.experimental.pallas import tpu as pltpu
from jax.sharding import PartitionSpec as P

MESH = pl.DeviceIdType.MESH
CHUNK = 16
ROWS = 256


def turn_kernel(
    shape, samples, gain, pfb_weights, chan_map, received,
    raw, cal, weights, filtered, table, partial, spectra,
    load_sem, halo_send, halo_recv, send_sem, recv_sem, own_sem,
):
    n_ta, n_ba, taps, frames, frame_len = shape
    n_dev = n_ta * n_ba
    half = CHUNK // 2
    before, after = taps - 1 - half, half
    ta, ba = lax.axis_index("ta"), lax.axis_index("ba")
    me = ta * n_ba + ba
    table_rows = table.shape[0]
    rows_dev = table_rows // n_dev
    blocks = table_rows // ROWS

    def load(index, first, count):
        return pltpu.make_async_copy(
            samples.at[pl.ds(first, count)], raw.at[pl.ds(first, count)], load_sem.at[index]
        )

    last = load(0, frames - before, before)
    first = load(1, 0, after)
    middle = load(2, after, frames - before - after)
    last.start()
    first.start()
    middle.start()

    barrier = pltpu.get_barrier_semaphore()

    @pl.loop(1, n_dev)
    def _(step):
        other = lax.rem(me + step, n_dev)
        pl.semaphore_signal(
            barrier, inc=1, device_id=(other // n_ba, lax.rem(other, n_ba)), device_id_type=MESH
        )

    def calibrate(start, count):
        pieces = frame_len // 256

        @pl.loop(0, count * pieces)
        def _(step):
            frame = start + step // pieces
            rows = pl.ds(pl.multiple_of(lax.rem(step, pieces) * 256, 256), 256)
            value = raw[frame, rows, :].astype(jnp.float32) * gain[...]
            cal[frame + before, rows, :] = value.astype(jnp.bfloat16)

    forward = pltpu.make_async_remote_copy(
        src_ref=cal.at[pl.ds(frames, before)],
        dst_ref=cal.at[pl.ds(0, before)],
        send_sem=halo_send.at[0],
        recv_sem=halo_recv.at[0],
        device_id=(jnp.minimum(ta + 1, n_ta - 1), ba),
        device_id_type=MESH,
    )
    backward = pltpu.make_async_remote_copy(
        src_ref=cal.at[pl.ds(before, after)],
        dst_ref=cal.at[pl.ds(before + frames, after)],
        send_sem=halo_send.at[1],
        recv_sem=halo_recv.at[1],
        device_id=(lax.rem(ta + n_ta - 1, n_ta), ba),
        device_id_type=MESH,
    )

    last.wait()
    calibrate(frames - before, before)
    pl.semaphore_wait(barrier, n_dev - 1)

    @pl.when(ta < n_ta - 1)
    def _():
        forward.start()

    first.wait()
    calibrate(0, after)
    backward.start()
    middle.wait()
    calibrate(after, frames - before - after)

    filler = jnp.zeros((128 - taps, frame_len), jnp.float32)
    weights[...] = jnp.concatenate([pfb_weights[...], filler], axis=0).T

    step_angle = 2.0 * math.pi / frame_len
    scale = 1.0 / math.sqrt(frame_len)
    chans = ROWS // 2

    def pair(turns):
        centred = ((turns + frame_len // 2) & (frame_len - 1)) - frame_len // 2
        angle = centred.astype(jnp.float32) * step_angle
        return jnp.cos(angle), jnp.sin(angle)

    lane = lax.broadcasted_iota(jnp.int32, (chans, 128), 1)
    for b in range(blocks):
        row = chan_map[:, b * chans : (b + 1) * chans].astype(jnp.float32)
        chan = jnp.broadcast_to(row, (128, chans)).T.astype(jnp.int32)
        fine_cos, fine_sin = pair(chan * lane)
        coarse_cos, coarse_sin = pair(chan * lane * 128)
        for a in range(frame_len // 128):
            cos_a = coarse_cos[:, a : a + 1] * scale
            sin_a = coarse_sin[:, a : a + 1] * scale
            columns = slice(a * 128, (a + 1) * 128)
            real = fine_cos * cos_a - fine_sin * sin_a
            imaginary = -(fine_sin * cos_a + fine_cos * sin_a)
            table[b * ROWS : b * ROWS + chans, columns] = real.astype(jnp.bfloat16)
            table[b * ROWS + chans : (b + 1) * ROWS, columns] = imaginary.astype(jnp.bfloat16)

    near_base = ta // (n_ta // 2) * (n_dev // 2)
    far_base = n_dev // 2 - near_base

    def message(q, dest):
        return pltpu.make_async_remote_copy(
            src_ref=spectra.at[q, pl.ds(dest * rows_dev, rows_dev)],
            dst_ref=received.at[q, me],
            send_sem=send_sem.at[q, dest],
            recv_sem=recv_sem.at[q, me],
            device_id=(dest // n_ba, lax.rem(dest, n_ba)),
            device_id_type=MESH,
        )

    def own(q):
        return pltpu.make_async_copy(
            spectra.at[q, pl.ds(me * rows_dev, rows_dev)], received.at[q, me], own_sem.at[q]
        )

    @pl.loop(0, 2)
    def _(q):
        @pl.when(jnp.logical_and(q == 1, ta > 0))
        def _():
            forward.wait_recv()

        @pl.when(jnp.logical_and(q == 1, ta == 0))
        def _():
            @pl.loop(0, before)
            def _(frame):
                cal[frame] = jnp.zeros((frame_len, 128), jnp.bfloat16)

        @pl.when(q == 1)
        def _():
            backward.wait_recv()

        @pl.when(jnp.logical_and(q == 1, ta == n_ta - 1))
        def _():
            @pl.loop(frames + before - taps + 1, frames + before)
            def _(frame):
                cal[frame] = jnp.zeros((frame_len, 128), jnp.bfloat16)

        @pl.loop(0, frame_len // 16)
        def _(block):
            rows = pl.ds(pl.multiple_of(block * 16, 16), 16)
            own_weights = weights[rows, :]
            taps_here = [jnp.broadcast_to(own_weights[:, t : t + 1], (16, 128)) for t in range(taps)]
            for group in range(CHUNK // 4):
                side = group * 4 // half
                lead = (1 - q) * (half + side * half) + q * side * (frames - half) + group * 4 - side * half
                sums = [None] * 4
                for f in range(taps + 3):
                    x = cal[lead + f, rows, :].astype(jnp.float32)
                    for j in range(4):
                        t = f - j
                        if 0 <= t < taps:
                            term = taps_here[t] * x
                            sums[j] = term if sums[j] is None else sums[j] + term
                for j in range(4):
                    s = group * 4 + j
                    filtered[s // 2, rows, (s % 2) * 128 : (s % 2 + 1) * 128] = sums[j].astype(jnp.bfloat16)

        @pl.loop(0, blocks)
        def _(b):
            base = pl.multiple_of(b * ROWS, ROWS)
            left = table[pl.ds(base, ROWS), :]

            @pl.loop(0, CHUNK // 2)
            def _(two):
                result = jnp.dot(left, filtered[two], preferred_element_type=jnp.float32)
                start = pl.multiple_of(two * 2 * ROWS, ROWS)
                partial[pl.ds(start, ROWS), :] = result[:, :128]
                partial[pl.ds(start + ROWS, ROWS), :] = result[:, 128:]

            @pl.loop(0, chans // 8)
            def _(c8):
                for r in range(8):
                    c = c8 * 8 + r
                    for p in range(2):
                        values = partial[pl.ds(c + p * chans, CHUNK, stride=ROWS), :]
                        spectra[q, base + 2 * c + p] = values.astype(jnp.bfloat16)

        @pl.loop(0, n_dev // 2)
        def _(j):
            place = lax.rem(me + j, n_dev // 2)
            message(q, far_base + place).start()
            dest = near_base + place

            @pl.when(dest != me)
            def _():
                message(q, dest).start()

            @pl.when(dest == me)
            def _():
                own(q).start()

    @pl.when(ta < n_ta - 1)
    def _():
        forward.wait_send()

    backward.wait_send()

    @pl.loop(0, 2)
    def _(q):
        own(q).wait()

        @pl.loop(1, n_dev)
        def _(step):
            other = lax.rem(me + step, n_dev)
            message(q, other).wait_send()
            pltpu.make_async_remote_copy(
                src_ref=spectra.at[q, pl.ds(other * rows_dev, rows_dev)],
                dst_ref=received.at[q, other],
                send_sem=send_sem.at[q, other],
                recv_sem=recv_sem.at[q, other],
                device_id=(other // n_ba, lax.rem(other, n_ba)),
                device_id_type=MESH,
            ).wait_recv()


def correlate_kernel(scale, received, out):
    n_chunks, n_ta, n_ba = received.shape[:3]
    depth = n_chunks * n_ta * received.shape[4]

    def part(row):
        return jnp.concatenate(
            [received[:, :, b, row].reshape(depth, 128) for b in range(n_ba)], axis=1
        )

    for c in range(out.shape[1]):
        re, im = part(2 * c), part(2 * c + 1)
        right = jnp.concatenate([re, im], axis=0)
        re_t, im_t = re.T, im.T
        out[0, c] = jnp.dot(jnp.concatenate([re_t, im_t], axis=1), right, preferred_element_type=jnp.float32) * scale
        out[1, c] = jnp.dot(jnp.concatenate([im_t, -re_t], axis=1), right, preferred_element_type=jnp.float32) * scale


def per_device(samples, input_gain, pfb_weights, chan_map):
    taps, frame_len = pfb_weights.shape
    frames = samples.shape[0] // frame_len
    n_ta, n_ba = lax.axis_size("ta"), lax.axis_size("ba")
    n_dev = n_ta * n_ba
    table_rows = 2 * chan_map.shape[0]
    rows_dev = table_rows // n_dev
    n_chunks = frames // CHUNK
    inputs = n_ba * samples.shape[1]
    vmem = pl.BlockSpec(memory_space=pltpu.VMEM)
    hbm = pl.BlockSpec(memory_space=pl.ANY)
    received = pl.pallas_call(
        functools.partial(turn_kernel, (n_ta, n_ba, taps, frames, frame_len)),
        out_shape=jax.ShapeDtypeStruct((n_chunks, n_dev, rows_dev, CHUNK, 128), jnp.bfloat16),
        in_specs=[hbm, vmem, vmem, vmem],
        out_specs=hbm,
        scratch_shapes=[
            pltpu.VMEM((frames, frame_len, 128), jnp.int32),
            pltpu.VMEM((frames + taps - 1, frame_len, 128), jnp.bfloat16),
            pltpu.VMEM((frame_len, 128), jnp.float32),
            pltpu.VMEM((CHUNK // 2, frame_len, 256), jnp.bfloat16),
            pltpu.VMEM((table_rows, frame_len), jnp.bfloat16),
            pltpu.VMEM((CHUNK * ROWS, 128), jnp.float32),
            pltpu.VMEM((n_chunks, table_rows, CHUNK, 128), jnp.bfloat16),
            pltpu.SemaphoreType.DMA((3,)),
            pltpu.SemaphoreType.DMA((2,)),
            pltpu.SemaphoreType.DMA((2,)),
            pltpu.SemaphoreType.DMA((n_chunks, n_dev)),
            pltpu.SemaphoreType.DMA((n_chunks, n_dev)),
            pltpu.SemaphoreType.DMA((n_chunks,)),
        ],
        compiler_params=pltpu.CompilerParams(
            collective_id=0, has_side_effects=True, vmem_limit_bytes=56 * 1024 * 1024
        ),
        name="filter_turn",
    )(samples.reshape(frames, frame_len, 128), input_gain[None, :], pfb_weights, chan_map[None, :])
    received = received.reshape(n_chunks, n_ta, n_ba, rows_dev, CHUNK, 128)
    channels_dev = rows_dev // 2
    return pl.pallas_call(
        functools.partial(correlate_kernel, 1.0 / (n_ta * frames)),
        grid=(channels_dev // 2,),
        out_shape=jax.ShapeDtypeStruct((2, channels_dev, inputs, inputs), jnp.float32),
        in_specs=[pl.BlockSpec((n_chunks, n_ta, n_ba, 4, CHUNK, 128), lambda c: (0, 0, 0, c, 0, 0))],
        out_specs=pl.BlockSpec((2, 2, inputs, inputs), lambda c: (0, c, 0, 0)),
        compiler_params=pltpu.CompilerParams(vmem_limit_bytes=48 * 1024 * 1024),
        name="correlate",
    )(received)


def solution(mesh):
    placed = (P("ta", "ba"), P("ba"), P(), P())
    return jax.shard_map(
        per_device,
        mesh=mesh,
        in_specs=placed,
        out_specs=P(None, ("ta", "ba"), None, None),
        check_vma=False,
    )
```

```python
import functools
import math

import jax
import jax.numpy as jnp
from jax import lax
from jax.experimental import pallas as pl
from jax.experimental.pallas import tpu as pltpu
from jax.sharding import PartitionSpec as P

MESH = pl.DeviceIdType.MESH
CHUNK = 16
ROWS = 256


def turn_kernel(
    shape, samples, gain, pfb_weights, chan_map, received,
    raw, cal, weights, filtered, table, partial, spectra,
    load_sem, halo_send, halo_recv, send_sem, recv_sem, own_sem,
):
    n_ta, n_ba, taps, frames, frame_len = shape
    n_dev = n_ta * n_ba
    half = CHUNK // 2
    before, after = taps - 1 - half, half
    ta, ba = lax.axis_index("ta"), lax.axis_index("ba")
    me = ta * n_ba + ba
    table_rows = table.shape[0]
    rows_dev = table_rows // n_dev
    blocks = table_rows // ROWS

    def load(index, first, count):
        return pltpu.make_async_copy(
            samples.at[pl.ds(first, count)], raw.at[pl.ds(first, count)], load_sem.at[index]
        )

    last = load(0, frames - before, before)
    first = load(1, 0, after)
    middle = load(2, after, frames - before - after)
    last.start()
    first.start()
    middle.start()

    barrier = pltpu.get_barrier_semaphore()

    @pl.loop(1, n_dev)
    def _(step):
        other = lax.rem(me + step, n_dev)
        pl.semaphore_signal(
            barrier, inc=1, device_id=(other // n_ba, lax.rem(other, n_ba)), device_id_type=MESH
        )

    def calibrate(start, count):
        pieces = frame_len // 256

        @pl.loop(0, count * pieces)
        def _(step):
            frame = start + step // pieces
            rows = pl.ds(pl.multiple_of(lax.rem(step, pieces) * 256, 256), 256)
            value = raw[frame, rows, :].astype(jnp.float32) * gain[...]
            cal[frame + before, rows, :] = value.astype(jnp.bfloat16)

    forward = pltpu.make_async_remote_copy(
        src_ref=cal.at[pl.ds(frames, before)],
        dst_ref=cal.at[pl.ds(0, before)],
        send_sem=halo_send.at[0],
        recv_sem=halo_recv.at[0],
        device_id=(jnp.minimum(ta + 1, n_ta - 1), ba),
        device_id_type=MESH,
    )
    backward = pltpu.make_async_remote_copy(
        src_ref=cal.at[pl.ds(before, after)],
        dst_ref=cal.at[pl.ds(before + frames, after)],
        send_sem=halo_send.at[1],
        recv_sem=halo_recv.at[1],
        device_id=(lax.rem(ta + n_ta - 1, n_ta), ba),
        device_id_type=MESH,
    )

    last.wait()
    calibrate(frames - before, before)
    pl.semaphore_wait(barrier, n_dev - 1)

    @pl.when(ta < n_ta - 1)
    def _():
        forward.start()

    first.wait()
    calibrate(0, after)
    backward.start()
    middle.wait()
    calibrate(after, frames - before - after)

    filler = jnp.zeros((128 - taps, frame_len), jnp.float32)
    weights[...] = jnp.concatenate([pfb_weights[...], filler], axis=0).T

    step_angle = 2.0 * math.pi / frame_len
    scale = 1.0 / math.sqrt(frame_len)
    chans = ROWS // 2

    def pair(turns):
        centred = ((turns + frame_len // 2) & (frame_len - 1)) - frame_len // 2
        angle = centred.astype(jnp.float32) * step_angle
        return jnp.cos(angle), jnp.sin(angle)

    lane = lax.broadcasted_iota(jnp.int32, (chans, 128), 1)
    for b in range(blocks):
        row = chan_map[:, b * chans : (b + 1) * chans].astype(jnp.float32)
        chan = jnp.broadcast_to(row, (128, chans)).T.astype(jnp.int32)
        fine_cos, fine_sin = pair(chan * lane)
        coarse_cos, coarse_sin = pair(chan * lane * 128)
        for a in range(frame_len // 128):
            cos_a = coarse_cos[:, a : a + 1] * scale
            sin_a = coarse_sin[:, a : a + 1] * scale
            columns = slice(a * 128, (a + 1) * 128)
            real = fine_cos * cos_a - fine_sin * sin_a
            imaginary = -(fine_sin * cos_a + fine_cos * sin_a)
            table[b * ROWS : b * ROWS + chans, columns] = real.astype(jnp.bfloat16)
            table[b * ROWS + chans : (b + 1) * ROWS, columns] = imaginary.astype(jnp.bfloat16)

    near_base = ta // (n_ta // 2) * (n_dev // 2)
    far_base = n_dev // 2 - near_base

    def message(q, dest):
        return pltpu.make_async_remote_copy(
            src_ref=spectra.at[q, pl.ds(dest * rows_dev, rows_dev)],
            dst_ref=received.at[q, me],
            send_sem=send_sem.at[q, dest],
            recv_sem=recv_sem.at[q, me],
            device_id=(dest // n_ba, lax.rem(dest, n_ba)),
            device_id_type=MESH,
        )

    def own(q):
        return pltpu.make_async_copy(
            spectra.at[q, pl.ds(me * rows_dev, rows_dev)], received.at[q, me], own_sem.at[q]
        )

    @pl.loop(0, 2)
    def _(q):
        @pl.when(jnp.logical_and(q == 1, ta == 0))
        def _():
            @pl.loop(0, before)
            def _(frame):
                cal[frame] = jnp.zeros((frame_len, 128), jnp.bfloat16)

        @pl.when(jnp.logical_and(q == 1, ta == n_ta - 1))
        def _():
            @pl.loop(frames + before - taps + 1, frames + before)
            def _(frame):
                cal[frame] = jnp.zeros((frame_len, 128), jnp.bfloat16)

        @pl.loop(0, frame_len // 16)
        def _(block):
            rows = pl.ds(pl.multiple_of(block * 16, 16), 16)
            own_weights = weights[rows, :]
            taps_here = [jnp.broadcast_to(own_weights[:, t : t + 1], (16, 128)) for t in range(taps)]
            for group in range(CHUNK // 4):
                side = group * 4 // half
                lead = (1 - q) * (half + side * half) + q * side * (frames - half) + group * 4 - side * half
                sums = [None] * 4
                for f in range(taps + 3):
                    x = cal[lead + f, rows, :].astype(jnp.float32)
                    for j in range(4):
                        t = f - j
                        if 0 <= t < taps:
                            term = taps_here[t] * x
                            sums[j] = term if sums[j] is None else sums[j] + term
                for j in range(4):
                    s = group * 4 + j
                    filtered[s // 2, rows, (s % 2) * 128 : (s % 2 + 1) * 128] = sums[j].astype(jnp.bfloat16)

        @pl.loop(0, blocks)
        def _(b):
            base = pl.multiple_of(b * ROWS, ROWS)
            left = table[pl.ds(base, ROWS), :]

            @pl.loop(0, CHUNK // 2)
            def _(two):
                result = jnp.dot(left, filtered[two], preferred_element_type=jnp.float32)
                start = pl.multiple_of(two * 2 * ROWS, ROWS)
                partial[pl.ds(start, ROWS), :] = result[:, :128]
                partial[pl.ds(start + ROWS, ROWS), :] = result[:, 128:]

            @pl.loop(0, chans // 8)
            def _(c8):
                for r in range(8):
                    c = c8 * 8 + r
                    for p in range(2):
                        values = partial[pl.ds(c + p * chans, CHUNK, stride=ROWS), :]
                        spectra[q, base + 2 * c + p] = values.astype(jnp.bfloat16)

        @pl.when(jnp.logical_and(q == 0, ta > 0))
        def _():
            forward.wait_recv()

        @pl.when(q == 0)
        def _():
            backward.wait_recv()

        @pl.loop(0, n_dev // 2)
        def _(j):
            place = lax.rem(me + j, n_dev // 2)
            message(q, far_base + place).start()

            @pl.when(q == 1)
            def _():
                dest = near_base + place

                @pl.when(dest != me)
                def _():
                    message(0, dest).start()
                    message(1, dest).start()

                @pl.when(dest == me)
                def _():
                    own(0).start()
                    own(1).start()

    @pl.when(ta < n_ta - 1)
    def _():
        forward.wait_send()

    backward.wait_send()

    @pl.loop(0, 2)
    def _(q):
        own(q).wait()

        @pl.loop(1, n_dev)
        def _(step):
            other = lax.rem(me + step, n_dev)
            message(q, other).wait_send()
            pltpu.make_async_remote_copy(
                src_ref=spectra.at[q, pl.ds(other * rows_dev, rows_dev)],
                dst_ref=received.at[q, other],
                send_sem=send_sem.at[q, other],
                recv_sem=recv_sem.at[q, other],
                device_id=(other // n_ba, lax.rem(other, n_ba)),
                device_id_type=MESH,
            ).wait_recv()


def correlate_kernel(scale, received, out):
    n_chunks, n_ta, n_ba = received.shape[:3]
    depth = n_chunks * n_ta * received.shape[4]

    def part(row):
        return jnp.concatenate(
            [received[:, :, b, row].reshape(depth, 128) for b in range(n_ba)], axis=1
        )

    for c in range(out.shape[1]):
        re, im = part(2 * c), part(2 * c + 1)
        right = jnp.concatenate([re, im], axis=0)
        re_t, im_t = re.T, im.T
        out[0, c] = jnp.dot(jnp.concatenate([re_t, im_t], axis=1), right, preferred_element_type=jnp.float32) * scale
        out[1, c] = jnp.dot(jnp.concatenate([im_t, -re_t], axis=1), right, preferred_element_type=jnp.float32) * scale


def per_device(samples, input_gain, pfb_weights, chan_map):
    taps, frame_len = pfb_weights.shape
    frames = samples.shape[0] // frame_len
    n_ta, n_ba = lax.axis_size("ta"), lax.axis_size("ba")
    n_dev = n_ta * n_ba
    table_rows = 2 * chan_map.shape[0]
    rows_dev = table_rows // n_dev
    n_chunks = frames // CHUNK
    inputs = n_ba * samples.shape[1]
    vmem = pl.BlockSpec(memory_space=pltpu.VMEM)
    hbm = pl.BlockSpec(memory_space=pl.ANY)
    received = pl.pallas_call(
        functools.partial(turn_kernel, (n_ta, n_ba, taps, frames, frame_len)),
        out_shape=jax.ShapeDtypeStruct((n_chunks, n_dev, rows_dev, CHUNK, 128), jnp.bfloat16),
        in_specs=[hbm, vmem, vmem, vmem],
        out_specs=hbm,
        scratch_shapes=[
            pltpu.VMEM((frames, frame_len, 128), jnp.int32),
            pltpu.VMEM((frames + taps - 1, frame_len, 128), jnp.bfloat16),
            pltpu.VMEM((frame_len, 128), jnp.float32),
            pltpu.VMEM((CHUNK // 2, frame_len, 256), jnp.bfloat16),
            pltpu.VMEM((table_rows, frame_len), jnp.bfloat16),
            pltpu.VMEM((CHUNK * ROWS, 128), jnp.float32),
            pltpu.VMEM((n_chunks, table_rows, CHUNK, 128), jnp.bfloat16),
            pltpu.SemaphoreType.DMA((3,)),
            pltpu.SemaphoreType.DMA((2,)),
            pltpu.SemaphoreType.DMA((2,)),
            pltpu.SemaphoreType.DMA((n_chunks, n_dev)),
            pltpu.SemaphoreType.DMA((n_chunks, n_dev)),
            pltpu.SemaphoreType.DMA((n_chunks,)),
        ],
        compiler_params=pltpu.CompilerParams(
            collective_id=0, has_side_effects=True, vmem_limit_bytes=56 * 1024 * 1024
        ),
        name="filter_turn",
    )(samples.reshape(frames, frame_len, 128), input_gain[None, :], pfb_weights, chan_map[None, :])
    received = received.reshape(n_chunks, n_ta, n_ba, rows_dev, CHUNK, 128)
    channels_dev = rows_dev // 2
    return pl.pallas_call(
        functools.partial(correlate_kernel, 1.0 / (n_ta * frames)),
        grid=(channels_dev // 2,),
        out_shape=jax.ShapeDtypeStruct((2, channels_dev, inputs, inputs), jnp.float32),
        in_specs=[pl.BlockSpec((n_chunks, n_ta, n_ba, 4, CHUNK, 128), lambda c: (0, 0, 0, c, 0, 0))],
        out_specs=pl.BlockSpec((2, 2, inputs, inputs), lambda c: (0, c, 0, 0)),
        compiler_params=pltpu.CompilerParams(vmem_limit_bytes=48 * 1024 * 1024),
        name="correlate",
    )(received)


def solution(mesh):
    placed = (P("ta", "ba"), P("ba"), P(), P())
    return jax.shard_map(
        per_device,
        mesh=mesh,
        in_specs=placed,
        out_specs=P(None, ("ta", "ba"), None, None),
        check_vma=False,
    )
```

```python
import functools
import math

import jax
import jax.numpy as jnp
from jax import lax
from jax.experimental import pallas as pl
from jax.experimental.pallas import tpu as pltpu
from jax.sharding import PartitionSpec as P

MESH = pl.DeviceIdType.MESH
CHUNK = 16
ROWS = 256


def turn_kernel(
    shape, samples, gain, pfb_weights, chan_map, received,
    raw, cal, weights, filtered, table, partial, spectra,
    load_sem, halo_send, halo_recv, send_sem, recv_sem, own_sem,
):
    n_ta, n_ba, taps, frames, frame_len = shape
    n_dev = n_ta * n_ba
    half = CHUNK // 2
    before, after = taps - 1 - half, half
    ta, ba = lax.axis_index("ta"), lax.axis_index("ba")
    me = ta * n_ba + ba
    table_rows = table.shape[0]
    rows_dev = table_rows // n_dev
    blocks = table_rows // ROWS
    dests = n_dev // blocks

    def load(index, first, count):
        return pltpu.make_async_copy(
            samples.at[pl.ds(first, count)], raw.at[pl.ds(first, count)], load_sem.at[index]
        )

    last = load(0, frames - before, before)
    first = load(1, 0, after)
    middle = load(2, after, frames - before - after)
    last.start()
    first.start()
    middle.start()

    barrier = pltpu.get_barrier_semaphore()

    @pl.loop(1, n_dev)
    def _(step):
        other = lax.rem(me + step, n_dev)
        pl.semaphore_signal(
            barrier, inc=1, device_id=(other // n_ba, lax.rem(other, n_ba)), device_id_type=MESH
        )

    def calibrate(start, count):
        pieces = frame_len // 256

        @pl.loop(0, count * pieces)
        def _(step):
            frame = start + step // pieces
            rows = pl.ds(pl.multiple_of(lax.rem(step, pieces) * 256, 256), 256)
            value = raw[frame, rows, :].astype(jnp.float32) * gain[...]
            cal[frame + before, rows, :] = value.astype(jnp.bfloat16)

    def halo_copy(index, source, target, count, shard):
        return pltpu.make_async_remote_copy(
            src_ref=cal.at[pl.ds(source, count)],
            dst_ref=cal.at[pl.ds(target, count)],
            send_sem=halo_send.at[index],
            recv_sem=halo_recv.at[index],
            device_id=(shard, ba),
            device_id_type=MESH,
        )

    after_me = jnp.minimum(ta + 1, n_ta - 1)
    before_me = lax.rem(ta + n_ta - 1, n_ta)
    cut = half // 2
    forward = [
        halo_copy(0, frames, 0, cut, after_me),
        halo_copy(1, frames + cut, cut, before - cut, after_me),
    ]
    backward = [
        halo_copy(2, before, before + frames, cut, before_me),
        halo_copy(3, before + cut, before + frames + cut, after - cut, before_me),
    ]

    last.wait()
    calibrate(frames - before, before)
    pl.semaphore_wait(barrier, n_dev - 1)

    @pl.when(ta < n_ta - 1)
    def _():
        for copy in forward:
            copy.start()

    first.wait()
    calibrate(0, after)
    for copy in backward:
        copy.start()
    middle.wait()
    calibrate(after, frames - before - after)

    filler = jnp.zeros((128 - taps, frame_len), jnp.float32)
    weights[...] = jnp.concatenate([pfb_weights[...], filler], axis=0).T

    step_angle = 2.0 * math.pi / frame_len
    scale = 1.0 / math.sqrt(frame_len)
    chans = ROWS // 2

    def pair(turns):
        centred = ((turns + frame_len // 2) & (frame_len - 1)) - frame_len // 2
        angle = centred.astype(jnp.float32) * step_angle
        return jnp.cos(angle), jnp.sin(angle)

    lane = lax.broadcasted_iota(jnp.int32, (chans, 128), 1)
    for b in range(blocks):
        row = chan_map[:, b * chans : (b + 1) * chans].astype(jnp.float32)
        chan = jnp.broadcast_to(row, (128, chans)).T.astype(jnp.int32)
        fine_cos, fine_sin = pair(chan * lane)
        coarse_cos, coarse_sin = pair(chan * lane * 128)
        for a in range(frame_len // 128):
            cos_a = coarse_cos[:, a : a + 1] * scale
            sin_a = coarse_sin[:, a : a + 1] * scale
            columns = slice(a * 128, (a + 1) * 128)
            real = fine_cos * cos_a - fine_sin * sin_a
            imaginary = -(fine_sin * cos_a + fine_cos * sin_a)
            table[b * ROWS : b * ROWS + chans, columns] = real.astype(jnp.bfloat16)
            table[b * ROWS + chans : (b + 1) * ROWS, columns] = imaginary.astype(jnp.bfloat16)

    lower = 1 - ta // (n_ta // 2)

    def message(q, dest):
        return pltpu.make_async_remote_copy(
            src_ref=spectra.at[q, pl.ds(dest * rows_dev, rows_dev)],
            dst_ref=received.at[q, me],
            send_sem=send_sem.at[q, dest],
            recv_sem=recv_sem.at[q, me],
            device_id=(dest // n_ba, lax.rem(dest, n_ba)),
            device_id_type=MESH,
        )

    def own(q):
        return pltpu.make_async_copy(
            spectra.at[q, pl.ds(me * rows_dev, rows_dev)], received.at[q, me], own_sem.at[q]
        )

    @pl.loop(0, 2)
    def _(q):
        @pl.when(jnp.logical_and(q == 1, ta > 0))
        def _():
            for copy in forward:
                copy.wait_recv()

        @pl.when(jnp.logical_and(q == 1, ta == 0))
        def _():
            @pl.loop(0, before)
            def _(frame):
                cal[frame] = jnp.zeros((frame_len, 128), jnp.bfloat16)

        @pl.when(q == 1)
        def _():
            for copy in backward:
                copy.wait_recv()

        @pl.when(jnp.logical_and(q == 1, ta == n_ta - 1))
        def _():
            @pl.loop(frames + before - taps + 1, frames + before)
            def _(frame):
                cal[frame] = jnp.zeros((frame_len, 128), jnp.bfloat16)

        @pl.loop(0, frame_len // 16)
        def _(block):
            rows = pl.ds(pl.multiple_of(block * 16, 16), 16)
            own_weights = weights[rows, :]
            taps_here = [jnp.broadcast_to(own_weights[:, t : t + 1], (16, 128)) for t in range(taps)]
            for group in range(CHUNK // 4):
                side = group * 4 // half
                lead = (1 - q) * (half + side * half) + q * side * (frames - half) + group * 4 - side * half
                sums = [None] * 4
                for f in range(taps + 3):
                    x = cal[lead + f, rows, :].astype(jnp.float32)
                    for j in range(4):
                        t = f - j
                        if 0 <= t < taps:
                            term = taps_here[t] * x
                            sums[j] = term if sums[j] is None else sums[j] + term
                for j in range(4):
                    s = group * 4 + j
                    filtered[s // 2, rows, (s % 2) * 128 : (s % 2 + 1) * 128] = sums[j].astype(jnp.bfloat16)

        @pl.loop(0, blocks)
        def _(p):
            b = p + (blocks - 1 - 2 * p) * lower
            base = pl.multiple_of(b * ROWS, ROWS)
            left = table[pl.ds(base, ROWS), :]

            @pl.loop(0, CHUNK // 2)
            def _(two):
                result = jnp.dot(left, filtered[two], preferred_element_type=jnp.float32)
                start = pl.multiple_of(two * 2 * ROWS, ROWS)
                partial[pl.ds(start, ROWS), :] = result[:, :128]
                partial[pl.ds(start + ROWS, ROWS), :] = result[:, 128:]

            @pl.loop(0, chans // 8)
            def _(c8):
                for r in range(8):
                    c = c8 * 8 + r
                    for p in range(2):
                        values = partial[pl.ds(c + p * chans, CHUNK, stride=ROWS), :]
                        spectra[q, base + 2 * c + p] = values.astype(jnp.bfloat16)

            @pl.loop(0, dests)
            def _(j):
                dest = b * dests + lax.rem(j + me, dests)

                @pl.when(dest != me)
                def _():
                    message(q, dest).start()

                @pl.when(dest == me)
                def _():
                    own(q).start()

    @pl.when(ta < n_ta - 1)
    def _():
        for copy in forward:
            copy.wait_send()

    for copy in backward:
        copy.wait_send()

    @pl.loop(0, 2)
    def _(q):
        own(q).wait()

        @pl.loop(1, n_dev)
        def _(step):
            other = lax.rem(me + step, n_dev)
            message(q, other).wait_send()
            pltpu.make_async_remote_copy(
                src_ref=spectra.at[q, pl.ds(other * rows_dev, rows_dev)],
                dst_ref=received.at[q, other],
                send_sem=send_sem.at[q, other],
                recv_sem=recv_sem.at[q, other],
                device_id=(other // n_ba, lax.rem(other, n_ba)),
                device_id_type=MESH,
            ).wait_recv()


def correlate_kernel(scale, received, out):
    n_chunks, n_ta, n_ba = received.shape[:3]
    depth = n_chunks * n_ta * received.shape[4]

    def part(row):
        return jnp.concatenate(
            [received[:, :, b, row].reshape(depth, 128) for b in range(n_ba)], axis=1
        )

    for c in range(out.shape[1]):
        re, im = part(2 * c), part(2 * c + 1)
        right = jnp.concatenate([re, im], axis=0)
        re_t, im_t = re.T, im.T
        out[0, c] = jnp.dot(jnp.concatenate([re_t, im_t], axis=1), right, preferred_element_type=jnp.float32) * scale
        out[1, c] = jnp.dot(jnp.concatenate([im_t, -re_t], axis=1), right, preferred_element_type=jnp.float32) * scale


def per_device(samples, input_gain, pfb_weights, chan_map):
    taps, frame_len = pfb_weights.shape
    frames = samples.shape[0] // frame_len
    n_ta, n_ba = lax.axis_size("ta"), lax.axis_size("ba")
    n_dev = n_ta * n_ba
    table_rows = 2 * chan_map.shape[0]
    rows_dev = table_rows // n_dev
    n_chunks = frames // CHUNK
    inputs = n_ba * samples.shape[1]
    vmem = pl.BlockSpec(memory_space=pltpu.VMEM)
    hbm = pl.BlockSpec(memory_space=pl.ANY)
    received = pl.pallas_call(
        functools.partial(turn_kernel, (n_ta, n_ba, taps, frames, frame_len)),
        out_shape=jax.ShapeDtypeStruct((n_chunks, n_dev, rows_dev, CHUNK, 128), jnp.bfloat16),
        in_specs=[hbm, vmem, vmem, vmem],
        out_specs=hbm,
        scratch_shapes=[
            pltpu.VMEM((frames, frame_len, 128), jnp.int32),
            pltpu.VMEM((frames + taps - 1, frame_len, 128), jnp.bfloat16),
            pltpu.VMEM((frame_len, 128), jnp.float32),
            pltpu.VMEM((CHUNK // 2, frame_len, 256), jnp.bfloat16),
            pltpu.VMEM((table_rows, frame_len), jnp.bfloat16),
            pltpu.VMEM((CHUNK * ROWS, 128), jnp.float32),
            pltpu.VMEM((n_chunks, table_rows, CHUNK, 128), jnp.bfloat16),
            pltpu.SemaphoreType.DMA((3,)),
            pltpu.SemaphoreType.DMA((4,)),
            pltpu.SemaphoreType.DMA((4,)),
            pltpu.SemaphoreType.DMA((n_chunks, n_dev)),
            pltpu.SemaphoreType.DMA((n_chunks, n_dev)),
            pltpu.SemaphoreType.DMA((n_chunks,)),
        ],
        compiler_params=pltpu.CompilerParams(
            collective_id=0, has_side_effects=True, vmem_limit_bytes=56 * 1024 * 1024
        ),
        name="filter_turn",
    )(samples.reshape(frames, frame_len, 128), input_gain[None, :], pfb_weights, chan_map[None, :])
    received = received.reshape(n_chunks, n_ta, n_ba, rows_dev, CHUNK, 128)
    channels_dev = rows_dev // 2
    return pl.pallas_call(
        functools.partial(correlate_kernel, 1.0 / (n_ta * frames)),
        grid=(channels_dev // 2,),
        out_shape=jax.ShapeDtypeStruct((2, channels_dev, inputs, inputs), jnp.float32),
        in_specs=[pl.BlockSpec((n_chunks, n_ta, n_ba, 4, CHUNK, 128), lambda c: (0, 0, 0, c, 0, 0))],
        out_specs=pl.BlockSpec((2, 2, inputs, inputs), lambda c: (0, c, 0, 0)),
        compiler_params=pltpu.CompilerParams(vmem_limit_bytes=48 * 1024 * 1024),
        name="correlate",
    )(received)


def solution(mesh):
    placed = (P("ta", "ba"), P("ba"), P(), P())
    return jax.shard_map(
        per_device,
        mesh=mesh,
        in_specs=placed,
        out_specs=P(None, ("ta", "ba"), None, None),
        check_vma=False,
    )
```
